32 devices in a mesh: depth: 4 (over x, core), row: 2 (over y), col: 4 (over z).
Axes of the slice: x: 2, y: 2, z: 4, core: 2. Of those that a mesh axis runs over, the one named last changes fastest.
Arguments:
- tokens: bfloat16 [96, 8192], P(('depth', 'row')), may hold values from -6 to 6
- out_grad: bfloat16 [96, 8192], P(('depth', 'row')), may hold values from -0.59765625 to 0.59765625
- gate_weight: bfloat16 [8192, 16384], P('depth', ('row', 'col')), may hold values from -0.0625 to 0.0625
- up_weight: bfloat16 [8192, 16384], P('depth', ('row', 'col')), may hold values from -0.0625 to 0.0625
- down_weight: bfloat16 [16384, 8192], P(('row', 'col'), 'depth'), may hold values from -0.046875 to 0.046875
Outputs:
- input_grad: bfloat16 [96, 8192], P(('depth', 'row', 'col'))
- gate_grad: bfloat16 [8192, 16384], P('depth', ('row', 'col'))
- up_grad: bfloat16 [8192, 16384], P('depth', ('row', 'col'))
- down_grad: bfloat16 [16384, 8192], P(('row', 'col'), 'depth')
The draws below stay inside these ranges and needn't reach their ends.
All inputs are finite; a program needn't handle non-finite values.
Results may differ from the reference program's by a relative error of at most 0.024.
Values may be sent and summed in bfloat16 or wider, within the bound.
A program may use at most 320 MiB of HBM per device.

```python
import jax
import jax.numpy as jnp
from jax import lax

D = 8192
FF = 16384
TOK_BLK = 12
TOKENS = 96
N_DEPTH = 4
N_ROW = 2


def levels(stream_key, dims, shards, low, largest):
    def one(dim, parts):
        steps = jax.random.uniform(jax.random.fold_in(jax.random.fold_in(stream_key, 6), dim), (parts,), jnp.float32, low / len(shards), largest / len(shards))
        return jnp.repeat(jnp.exp(steps), dims[dim] // parts).reshape((-1,) + (1,) * (len(dims) - dim - 1))

    loudness = one(*shards[0])
    for cut in shards[1:]:
        loudness = loudness * one(*cut)
    return loudness


def noise(stream_key, extent, scale, bound, cuts=(), kind=jnp.bfloat16):
    values = scale * jax.random.normal(stream_key, extent, jnp.float32)
    if cuts:
        values = values * levels(stream_key, extent, cuts, -0.22, 0.18)
    return jnp.clip(values, -bound, bound).astype(kind)


def setup_inputs(seed: int = 0) -> dict:
    keys = jax.random.split(jax.random.key(seed), 6)
    tokens = noise(keys[0], (TOKENS, D), 1.0, 6.0, ((0, 8),))
    out_grad = noise(keys[1], (TOKENS, D), 0.1, 0.59765625, ((0, 8),))
    gate_weight = noise(keys[2], (D, FF), D ** -0.5, 0.0625, ((0, 4), (1, 8)))
    up_weight = noise(keys[3], (D, FF), D ** -0.5, 0.0625, ((0, 4), (1, 8)))
    down_weight = noise(keys[4], (FF, D), FF ** -0.5, 0.046875, ((0, 8), (1, 4)))
    return dict(tokens=tokens, out_grad=out_grad, gate_weight=gate_weight, up_weight=up_weight, down_weight=down_weight)


def contract_rows(left, right):
    return lax.dot_general(left, right, (((0,), (0,)), ((), ())), preferred_element_type=jnp.float32)


def contract_cols(left, right):
    return lax.dot_general(left, right, (((1,), (1,)), ((), ())), preferred_element_type=jnp.float32)


def reference(tokens, out_grad, gate_weight, up_weight, down_weight):
    gate = jnp.dot(tokens, gate_weight, preferred_element_type=jnp.float32)
    up = jnp.dot(tokens, up_weight, preferred_element_type=jnp.float32)
    sig = jax.nn.sigmoid(gate)
    act = gate * sig
    hidden = (act * up).astype(jnp.bfloat16)
    hidden_grad = contract_cols(out_grad, down_weight)
    gate_term = (hidden_grad * up * sig * (1.0 + gate * (1.0 - sig))).astype(jnp.bfloat16)
    up_term = (hidden_grad * act).astype(jnp.bfloat16)
    input_grad = contract_cols(gate_term, gate_weight) + contract_cols(up_term, up_weight)
    group = TOK_BLK * N_ROW
    gate_total = jnp.zeros(gate_weight.shape, jnp.float32)
    up_total = jnp.zeros(up_weight.shape, jnp.float32)
    down_total = jnp.zeros(down_weight.shape, jnp.float32)
    for k in range(N_DEPTH):
        lo = k * group
        tok_part = tokens[lo:lo + group]
        gate_total = gate_total + contract_rows(tok_part, gate_term[lo:lo + group]).astype(jnp.bfloat16).astype(jnp.float32)
        up_total = up_total + contract_rows(tok_part, up_term[lo:lo + group]).astype(jnp.bfloat16).astype(jnp.float32)
        down_total = down_total + contract_rows(hidden[lo:lo + group], out_grad[lo:lo + group]).astype(jnp.bfloat16).astype(jnp.float32)
    return (input_grad.astype(jnp.bfloat16), gate_total.astype(jnp.bfloat16),
            up_total.astype(jnp.bfloat16), down_total.astype(jnp.bfloat16))
```

```python
import functools

import jax
import jax.numpy as jnp
import numpy as np
from jax import lax
from jax.experimental import pallas as pl
from jax.experimental.pallas import tpu as pltpu
from jax.sharding import PartitionSpec as P


def contract_rows(left, right):
    return lax.dot_general(
        left, right, (((0,), (0,)), ((), ())), preferred_element_type=jnp.float32
    )


def contract_cols(left, right):
    return lax.dot_general(
        left, right, (((1,), (1,)), ((), ())), preferred_element_type=jnp.float32
    )


def swiglu_terms(gate, up, hidden_grad):
    sig = jax.nn.sigmoid(gate)
    act = gate * sig
    hidden = (act * up).astype(jnp.bfloat16)
    gate_term = (hidden_grad * up * sig * (1.0 + gate * (1.0 - sig))).astype(jnp.bfloat16)
    up_term = (hidden_grad * act).astype(jnp.bfloat16)
    return (hidden, gate_term, up_term)


def weight_stationary(n_depth, n_row, n_col):
    def on_device(tokens, out_grad, gate_weight, up_weight, down_weight):
        blk = tokens.shape[0]
        both = jnp.stack([tokens, out_grad])
        both = lax.all_to_all(both, "depth", split_axis=2, concat_axis=1, tiled=True)
        both = lax.all_gather(both, "row", axis=1, tiled=True)
        tok, grad = both[0], both[1]
        partial = jnp.stack(
            [
                jnp.dot(tok, gate_weight, preferred_element_type=jnp.float32),
                jnp.dot(tok, up_weight, preferred_element_type=jnp.float32),
                contract_cols(grad, down_weight),
            ]
        )
        sums = lax.psum_scatter(partial, "depth", scatter_dimension=1, tiled=True)
        terms = jnp.stack(swiglu_terms(sums[0], sums[1], sums[2]))
        hidden, gate_term, up_term = lax.all_gather(terms, "depth", axis=1, tiled=True)
        partial_in = contract_cols(gate_term, gate_weight) + contract_cols(up_term, up_weight)
        width = partial_in.shape[1]
        own = blk // n_col
        partial_in = partial_in.reshape(n_row, n_depth, n_col, own, width)
        partial_in = partial_in.transpose(0, 2, 1, 3, 4).reshape(-1, width)
        input_grad = lax.psum_scatter(
            partial_in, ("row", "col"), scatter_dimension=0, tiled=True
        ).astype(jnp.bfloat16)
        input_grad = lax.all_to_all(
            input_grad, "depth", split_axis=0, concat_axis=1, tiled=True
        )
        return (
            input_grad,
            contract_rows(tok, gate_term).astype(jnp.bfloat16),
            contract_rows(tok, up_term).astype(jnp.bfloat16),
            contract_rows(hidden, grad).astype(jnp.bfloat16),
        )

    return on_device


MESH = pl.DeviceIdType.MESH
CHUNK = 256
BF = jnp.bfloat16


def order_tokens(n_depth, n_row, n_col, own, cuts):
    blk = n_col * own
    rows = n_depth * n_row * blk
    out = np.zeros((cuts * 2 * rows, cuts * 2 * rows), np.float32)
    for cut in range(cuts):
        for a in range(2):
            for r in range(n_row):
                for c in range(n_col):
                    for d in range(n_depth):
                        for t in range(own):
                            to = ((r * n_col + c) * n_depth + d) * own + t
                            at = (((d * n_row + r) * cuts + cut) * 2 + a) * blk + c * own + t
                            out[(cut * 2 + a) * rows + to, at] = 1.0
    return out


def order_owners(n_depth, n_col, own, groups):
    out = np.zeros((n_depth * n_col * 16, groups * n_col * n_depth * own), np.float32)
    for d in range(n_depth):
        for c in range(n_col):
            for g in range(groups):
                for t in range(own):
                    out[(d * n_col + c) * 16 + g * own + t, ((g * n_col + c) * n_depth + d) * own + t] = 1.0
    return out


def chain_kernel(
    n_chunk,
    pk, wg_hbm, wu_hbm, wd_hbm, sel, sel_owner,
    tok_out, grad_out, terms_out, ig_out,
    wg, wu, wd, arrived, tok, grad, keep, core_snd, core_rcv, x_snd, x_rcv, terms, y,
    y_snd, y_rcv, z_snd, z_rcv, f_snd, f_rcv,
    w_sem, a_send, a_recv, a_sem, c_send, c_recv, x_send, x_recv, t_send, t_recv,
    y_send, y_recv, z_send, z_recv, f_send, f_recv, f_sem, o_sem,
):
    d, r, c = lax.axis_index("depth"), lax.axis_index("row"), lax.axis_index("col")
    core, chip = lax.rem(d, 2), lax.div(d, 2)
    mate = d + 1 - 2 * core
    across = d + 2 - 4 * chip
    width = wg.shape[0]
    cw = CHUNK
    half = tok.shape[0] // 2
    zw = width // 4

    def cols_of(j):
        return pl.ds(pl.multiple_of(j * cw, cw), cw)

    def w_copies(j):
        cols = cols_of(j)
        return (
            pltpu.make_async_copy(wg_hbm.at[:, cols], wg.at[:, cols], w_sem.at[0, j]),
            pltpu.make_async_copy(wu_hbm.at[:, cols], wu.at[:, cols], w_sem.at[1, j]),
            pltpu.make_async_copy(wd_hbm.at[cols, :], wd.at[cols, :], w_sem.at[2, j]),
        )

    for j in range(n_chunk):
        for cp in w_copies(j):
            cp.start()

    barrier = pltpu.get_barrier_semaphore()
    me8 = d * 2 + r
    for o in range(1, 8):
        to = lax.rem(me8 + o, 8)
        pl.semaphore_signal(barrier, inc=1, device_id=(lax.div(to, 2), lax.rem(to, 2), c), device_id_type=MESH)
    for oc in range(1, 4):
        for od in range(4):
            pl.semaphore_signal(barrier, inc=1, device_id=(lax.rem(d + od, 4), r, lax.rem(c + oc, 4)), device_id_type=MESH)
    pl.semaphore_wait(barrier, 19)

    blk = pk.shape[1]
    mine = pl.ds(pl.multiple_of(me8 * blk, blk), blk)
    a_copies = []
    for o in range(1, 8):
        to = lax.rem(me8 + o, 8)
        to_d, to_r = lax.div(to, 2), lax.rem(to, 2)
        a_copies.append(pltpu.make_async_remote_copy(
            pk.at[to_d], arrived.at[mine, :], a_send.at[o], a_recv.at[o],
            device_id=(to_d, to_r, c), device_id_type=MESH))
    for cp in a_copies:
        cp.start()
    own_copy = pltpu.make_async_copy(pk.at[d], arrived.at[mine, :], a_sem)
    own_copy.start()
    own_copy.wait()
    y[...] = jnp.zeros_like(y)
    for o in range(1, 8):
        frm = lax.rem(me8 + 8 - o, 8)
        rows = pl.ds(pl.multiple_of(frm * blk, blk), blk)
        pltpu.make_async_remote_copy(
            pk.at[0], arrived.at[rows, :], a_send.at[o], a_recv.at[o],
            device_id=(mate, r, c), device_id_type=MESH).wait_recv()

    n_tok = tok.shape[0]
    part = arrived.shape[1]
    for cut in range(width // part):
        for a, ref in ((0, tok), (1, grad)):
            at = (cut * 2 + a) * n_tok
            ref[:, cut * part:(cut + 1) * part] = jnp.dot(
                sel[at:at + n_tok, :], arrived[...], preferred_element_type=jnp.float32
            ).astype(BF)
    out_copies = [
        pltpu.make_async_copy(tok, tok_out, o_sem.at[0]),
        pltpu.make_async_copy(grad, grad_out, o_sem.at[1]),
    ]
    for cp in out_copies:
        cp.start()

    own_rows = pl.ds(pl.multiple_of(core * half, half), half)
    mate_rows = pl.ds(pl.multiple_of((1 - core) * half, half), half)

    def core_copy(j):
        return pltpu.make_async_remote_copy(
            core_snd.at[j], core_rcv.at[j], c_send.at[j], c_recv.at[j],
            device_id=(mate, r, c), device_id_type=MESH)

    def x_copy(j):
        return pltpu.make_async_remote_copy(
            x_snd.at[j], x_rcv.at[j], x_send.at[j], x_recv.at[j],
            device_id=(across, r, c), device_id_type=MESH)

    def t_copy(j, rows):
        return pltpu.make_async_remote_copy(
            terms.at[:, rows, cols_of(j)], terms.at[:, rows, cols_of(j)],
            t_send.at[j], t_recv.at[j], device_id=(mate, r, c), device_id_type=MESH)

    def forward(j):
        for cp in w_copies(j):
            cp.wait()
        cols = cols_of(j)
        sums = (
            jnp.dot(tok[...], wg[:, cols], preferred_element_type=jnp.float32),
            jnp.dot(tok[...], wu[:, cols], preferred_element_type=jnp.float32),
            contract_cols(grad[...], wd[cols, :]),
        )
        for k, p in enumerate(sums):
            low, high = p[:half], p[half:]
            keep[j, k] = jnp.where(core == 0, low, high)
            core_snd[j, k] = jnp.where(core == 0, high, low).astype(BF)
        core_copy(j).start()

    def chip_sum(j):
        core_copy(j).wait_recv()
        total = keep[j] + core_rcv[j].astype(jnp.float32)
        keep[j] = total
        x_snd[j] = total.astype(BF)
        x_copy(j).start()

    def finish(j):
        x_copy(j).wait_recv()
        total = keep[j] + x_rcv[j].astype(jnp.float32)
        for k, v in enumerate(swiglu_terms(total[0], total[1], total[2])):
            terms[k, own_rows, cols_of(j)] = v
        t_copy(j, own_rows).start()

    def input_sums(j):
        t_copy(j, mate_rows).wait_recv()
        cols = cols_of(j)
        gate_term, up_term = terms[1, :, cols], terms[2, :, cols]
        for n in range(4):
            rows = slice(n * zw, (n + 1) * zw)
            y[:, rows] += contract_cols(gate_term, wg[rows, cols]) + contract_cols(up_term, wu[rows, cols])

    def step(s, _):
        pl.when(s < n_chunk)(lambda: forward(s))
        pl.when((s >= 1) & (s < n_chunk + 1))(lambda: chip_sum(s - 1))
        pl.when((s >= 2) & (s < n_chunk + 2))(lambda: finish(s - 2))
        pl.when(s >= 3)(lambda: input_sums(s - 3))
        return 0

    lax.fori_loop(0, n_chunk + 3, step, 0)
    terms_copy = pltpu.make_async_copy(terms, terms_out, o_sem.at[2])
    terms_copy.start()

    def y_copy(o):
        return pltpu.make_async_remote_copy(
            y_snd.at[o], y_rcv.at[o], y_send.at[o], y_recv.at[o],
            device_id=(d, 1 - r, c), device_id_type=MESH)

    def z_copy(o):
        return pltpu.make_async_remote_copy(
            z_snd.at[o], z_rcv.at[o], z_send.at[o], z_recv.at[o],
            device_id=(d, r, lax.rem(c + o, 4)), device_id_type=MESH)

    row_own = pl.ds(pl.multiple_of(r * half, half), half)
    row_other = pl.ds(pl.multiple_of((1 - r) * half, half), half)

    def z_cols(o):
        return pl.ds(pl.multiple_of(lax.rem(c + o, 4) * zw, zw), zw)

    for o in (2, 1, 3, 0):
        y_snd[o] = y[row_other, z_cols(o)].astype(BF)
        y_copy(o).start()
    for o in (2, 1, 3):
        y_copy(o).wait_recv()
        z_snd[o] = (y[row_own, z_cols(o)] + y_rcv[o].astype(jnp.float32)).astype(BF)
        z_copy(o).start()
    y_copy(0).wait_recv()
    acc = y[row_own, z_cols(0)] + y_rcv[0].astype(jnp.float32)
    for o in (1, 3, 2):
        z_copy(o).wait_recv()
        acc = acc + z_rcv[o].astype(jnp.float32)
    acc = acc.astype(BF)
    stacked = jnp.concatenate([acc[:, g * 128:(g + 1) * 128] for g in range(zw // 128)], axis=0)
    owners = jnp.dot(sel_owner[...], stacked, preferred_element_type=jnp.float32).astype(BF)
    f_snd[...] = owners.reshape(f_snd.shape)

    me16 = d * 4 + c

    def f_copy(o):
        to = lax.rem(me16 + o, 16)
        return pltpu.make_async_remote_copy(
            f_snd.at[to], f_rcv.at[me16], f_send.at[o], f_recv.at[o],
            device_id=(lax.div(to, 4), r, lax.rem(to, 4)), device_id_type=MESH)

    for o in range(1, 16):
        f_copy(o).start()
    f_own = pltpu.make_async_copy(f_snd.at[me16], f_rcv.at[me16], f_sem)
    f_own.start()
    f_own.wait()
    for o in range(1, 16):
        frm = lax.rem(me16 + 16 - o, 16)
        pltpu.make_async_remote_copy(
            f_snd.at[0], f_rcv.at[frm], f_send.at[o], f_recv.at[o],
            device_id=(mate, r, c), device_id_type=MESH).wait_recv()
    ig_out[...] = f_rcv[...]

    for cp in a_copies:
        cp.wait_send()

    def drain(j, _):
        core_copy(j).wait_send()
        x_copy(j).wait_send()
        t_copy(j, own_rows).wait_send()
        return 0

    lax.fori_loop(0, n_chunk, drain, 0)
    for o in range(4):
        y_copy(o).wait_send()
    for o in range(1, 4):
        z_copy(o).wait_send()
    for o in range(1, 16):
        f_copy(o).wait_send()
    for cp in out_copies:
        cp.wait()
    terms_copy.wait()


def fused(n_depth, n_row, n_col):
    def on_device(tokens, out_grad, gate_weight, up_weight, down_weight):
        blk, model = tokens.shape
        width, units = gate_weight.shape
        own = blk // n_col
        n_tok = n_depth * n_row * blk
        cuts, part = 2, width // 2
        n_chunk = units // CHUNK
        half = n_tok // 2
        zw = width // n_col
        groups = zw // 128
        pk = jnp.stack([tokens, out_grad]).reshape(2, blk, n_depth, cuts, part)
        pk = pk.transpose(2, 3, 0, 1, 4).reshape(n_depth, cuts * 2 * blk, part)
        sel = jnp.asarray(order_tokens(n_depth, n_row, n_col, own, cuts), BF)
        sel_owner = jnp.asarray(order_owners(n_depth, n_col, own, groups), BF)
        sel_owner = sel_owner.reshape(n_depth * n_col * 16, -1)
        vmem, hbm = pl.BlockSpec(memory_space=pltpu.VMEM), pl.BlockSpec(memory_space=pl.ANY)
        dma = pltpu.SemaphoreType.DMA
        tok, grad, terms, ig = pl.pallas_call(
            functools.partial(chain_kernel, n_chunk),
            out_shape=(
                jax.ShapeDtypeStruct((n_tok, width), BF),
                jax.ShapeDtypeStruct((n_tok, width), BF),
                jax.ShapeDtypeStruct((3, n_tok, units), BF),
                jax.ShapeDtypeStruct((16, 16, 128), BF),
            ),
            in_specs=[vmem, hbm, hbm, hbm, vmem, vmem],
            out_specs=(hbm, hbm, hbm, vmem),
            scratch_shapes=[
                pltpu.VMEM((width, units), BF),
                pltpu.VMEM((width, units), BF),
                pltpu.VMEM((units, width), BF),
                pltpu.VMEM((n_depth * n_row * cuts * 2 * blk, part), BF),
                pltpu.VMEM((n_tok, width), BF),
                pltpu.VMEM((n_tok, width), BF),
                pltpu.VMEM((n_chunk, 3, half, CHUNK), jnp.float32),
                pltpu.VMEM((n_chunk, 3, half, CHUNK), BF),
                pltpu.VMEM((n_chunk, 3, half, CHUNK), BF),
                pltpu.VMEM((n_chunk, 3, half, CHUNK), BF),
                pltpu.VMEM((n_chunk, 3, half, CHUNK), BF),
                pltpu.VMEM((3, n_tok, units), BF),
                pltpu.VMEM((n_tok, width), jnp.float32),
                pltpu.VMEM((4, half, zw), BF),
                pltpu.VMEM((4, half, zw), BF),
                pltpu.VMEM((4, half, zw), BF),
                pltpu.VMEM((4, half, zw), BF),
                pltpu.VMEM((16, 16, 128), BF),
                pltpu.VMEM((16, 16, 128), BF),
                dma((3, n_chunk)),
                dma((8,)), dma((8,)), dma,
                dma((n_chunk,)), dma((n_chunk,)),
                dma((n_chunk,)), dma((n_chunk,)),
                dma((n_chunk,)), dma((n_chunk,)),
                dma((4,)), dma((4,)),
                dma((4,)), dma((4,)),
                dma((16,)), dma((16,)), dma,
                dma((3,)),
            ],
            compiler_params=pltpu.CompilerParams(
                collective_id=0, has_side_effects=True, vmem_limit_bytes=56 * 1024 * 1024
            ),
            cost_estimate=pl.CostEstimate(
                flops=10 * n_tok * width * units, bytes_accessed=6 * width * units, transcendentals=n_tok * units
            ),
        )(pk, gate_weight, up_weight, down_weight, sel, sel_owner)
        ig = ig.reshape(n_depth, n_col, 16, 128)[:, :, :groups * own]
        ig = ig.reshape(n_depth, n_col, groups, own, 128).transpose(3, 0, 1, 2, 4)
        return (
            ig.reshape(own, model),
            contract_rows(tok, terms[1]).astype(BF),
            contract_rows(tok, terms[2]).astype(BF),
            contract_rows(terms[0], grad).astype(BF),
        )

    return on_device


def solution(mesh):
    sizes = mesh.shape
    shape = (sizes["depth"], sizes["row"], sizes["col"])
    on_device = fused(*shape) if shape == (4, 2, 4) else weight_stationary(*shape)
    return jax.shard_map(
        on_device,
        mesh=mesh,
        in_specs=(
            P(("depth", "row"), None),
            P(("depth", "row"), None),
            P("depth", ("row", "col")),
            P("depth", ("row", "col")),
            P(("row", "col"), "depth"),
        ),
        out_specs=(
            P(("depth", "row", "col"), None),
            P("depth", ("row", "col")),
            P("depth", ("row", "col")),
            P(("row", "col"), "depth"),
        ),
        check_vma=False,
    )
```

```python
import functools

import jax
import jax.numpy as jnp
import numpy as np
from jax import lax
from jax.experimental import pallas as pl
from jax.experimental.pallas import tpu as pltpu
from jax.sharding import PartitionSpec as P


def contract_rows(left, right):
    return lax.dot_general(
        left, right, (((0,), (0,)), ((), ())), preferred_element_type=jnp.float32
    )


def contract_cols(left, right):
    return lax.dot_general(
        left, right, (((1,), (1,)), ((), ())), preferred_element_type=jnp.float32
    )


def swiglu_terms(gate, up, hidden_grad):
    sig = jax.nn.sigmoid(gate)
    act = gate * sig
    hidden = (act * up).astype(jnp.bfloat16)
    gate_term = (hidden_grad * up * sig * (1.0 + gate * (1.0 - sig))).astype(jnp.bfloat16)
    up_term = (hidden_grad * act).astype(jnp.bfloat16)
    return (hidden, gate_term, up_term)


def weight_stationary(n_depth, n_row, n_col):
    def on_device(tokens, out_grad, gate_weight, up_weight, down_weight):
        blk = tokens.shape[0]
        both = jnp.stack([tokens, out_grad])
        both = lax.all_to_all(both, "depth", split_axis=2, concat_axis=1, tiled=True)
        both = lax.all_gather(both, "row", axis=1, tiled=True)
        tok, grad = both[0], both[1]
        partial = jnp.stack(
            [
                jnp.dot(tok, gate_weight, preferred_element_type=jnp.float32),
                jnp.dot(tok, up_weight, preferred_element_type=jnp.float32),
                contract_cols(grad, down_weight),
            ]
        )
        sums = lax.psum_scatter(partial, "depth", scatter_dimension=1, tiled=True)
        terms = jnp.stack(swiglu_terms(sums[0], sums[1], sums[2]))
        hidden, gate_term, up_term = lax.all_gather(terms, "depth", axis=1, tiled=True)
        partial_in = contract_cols(gate_term, gate_weight) + contract_cols(up_term, up_weight)
        width = partial_in.shape[1]
        own = blk // n_col
        partial_in = partial_in.reshape(n_row, n_depth, n_col, own, width)
        partial_in = partial_in.transpose(0, 2, 1, 3, 4).reshape(-1, width)
        input_grad = lax.psum_scatter(
            partial_in, ("row", "col"), scatter_dimension=0, tiled=True
        ).astype(jnp.bfloat16)
        input_grad = lax.all_to_all(
            input_grad, "depth", split_axis=0, concat_axis=1, tiled=True
        )
        return (
            input_grad,
            contract_rows(tok, gate_term).astype(jnp.bfloat16),
            contract_rows(tok, up_term).astype(jnp.bfloat16),
            contract_rows(hidden, grad).astype(jnp.bfloat16),
        )

    return on_device


MESH = pl.DeviceIdType.MESH
CHUNK = 256
BF = jnp.bfloat16


def order_tokens(n_depth, n_row, n_col, own, cuts):
    blk = n_col * own
    rows = n_depth * n_row * blk
    out = np.zeros((cuts * rows, cuts * rows), np.float32)
    for cut in range(cuts):
        for r in range(n_row):
            for c in range(n_col):
                for d in range(n_depth):
                    for t in range(own):
                        to = ((r * n_col + c) * n_depth + d) * own + t
                        out[cut * rows + to, ((d * n_row + r) * cuts + cut) * blk + c * own + t] = 1.0
    return out


def order_owners(n_depth, n_col, own, groups):
    out = np.zeros((n_depth * n_col * 16, groups * n_col * n_depth * own), np.float32)
    for d in range(n_depth):
        for c in range(n_col):
            for g in range(groups):
                for t in range(own):
                    out[(d * n_col + c) * 16 + g * own + t, ((g * n_col + c) * n_depth + d) * own + t] = 1.0
    return out


def chain_kernel(
    n_chunk,
    tok_in, grad_in, wg_hbm, wu_hbm, wd_hbm, sel, sel_owner,
    tok_out, grad_out, terms_out, ig_out,
    pk, stage, wg, wu, wd, arrived, tok, grad, keep, core_snd, core_rcv, x_snd, x_rcv, terms, y,
    y_snd, y_rcv, z_snd, z_rcv, f_snd, f_rcv,
    w_sem, a_send, a_recv, a_sem, c_send, c_recv, x_send, x_recv, t_send, t_recv,
    y_send, y_recv, z_send, z_recv, f_send, f_recv, f_sem, o_sem,
):
    d, r, c = lax.axis_index("depth"), lax.axis_index("row"), lax.axis_index("col")
    core, chip = lax.rem(d, 2), lax.div(d, 2)
    mate = d + 1 - 2 * core
    across = d + 2 - 4 * chip
    width = wg.shape[0]
    cw = CHUNK
    half = tok.shape[0] // 2
    zw = width // 4

    def cols_of(j):
        return pl.ds(pl.multiple_of(j * cw, cw), cw)

    def w_copy(j, k):
        cols = cols_of(j)
        at = (cols, slice(None)) if k == 2 else (slice(None), cols)
        src, dst = ((wg_hbm, wg), (wu_hbm, wu), (wd_hbm, wd))[k]
        return pltpu.make_async_copy(src.at[at], dst.at[at], w_sem.at[k, j])

    for k in ((0, 1), (2,)):
        for j in range(n_chunk):
            for i in k:
                w_copy(j, i).start()

    barrier = pltpu.get_barrier_semaphore()
    me8 = d * 2 + r
    for o in range(1, 8):
        to = lax.rem(me8 + o, 8)
        pl.semaphore_signal(barrier, inc=1, device_id=(lax.div(to, 2), lax.rem(to, 2), c), device_id_type=MESH)
    for oc in range(1, 4):
        for od in range(4):
            pl.semaphore_signal(barrier, inc=1, device_id=(lax.rem(d + od, 4), r, lax.rem(c + oc, 4)), device_id_type=MESH)
    blk, part = pk.shape[2:]
    cuts = width // part
    own_blk = blk // cuts
    for a, ref in ((0, tok_in), (1, grad_in)):
        for q in range(4):
            for h in range(cuts):
                at = q * width + h * part
                stage[h * own_blk:(h + 1) * own_blk, :] = ref[:, at:at + part].astype(jnp.float32)
            pk[a, q] = stage[...].astype(BF)
    y[...] = jnp.zeros_like(y)
    pl.semaphore_wait(barrier, 19)

    mine = pl.ds(pl.multiple_of(me8 * blk, blk), blk)
    a_copies = []
    for a in range(2):
        for o in range(1, 8):
            to = lax.rem(me8 + o, 8)
            to_d, to_r = lax.div(to, 2), lax.rem(to, 2)
            a_copies.append(pltpu.make_async_remote_copy(
                pk.at[a, to_d], arrived.at[a, mine, :], a_send.at[a, o], a_recv.at[a, o],
                device_id=(to_d, to_r, c), device_id_type=MESH))
    for cp in a_copies:
        cp.start()
    own_copies = [pltpu.make_async_copy(pk.at[a, d], arrived.at[a, mine, :], a_sem.at[a]) for a in range(2)]
    for cp in own_copies:
        cp.start()
    n_tok = tok.shape[0]

    def take(a, ref, out):
        own_copies[a].wait()
        for o in range(1, 8):
            frm = lax.rem(me8 + 8 - o, 8)
            rows = pl.ds(pl.multiple_of(frm * blk, blk), blk)
            pltpu.make_async_remote_copy(
                pk.at[a, 0], arrived.at[a, rows, :], a_send.at[a, o], a_recv.at[a, o],
                device_id=(mate, r, c), device_id_type=MESH).wait_recv()
        for h in range(cuts):
            ref[:, h * part:(h + 1) * part] = jnp.dot(
                sel[h * n_tok:(h + 1) * n_tok, :], arrived[a], preferred_element_type=jnp.float32
            ).astype(BF)
        cp = pltpu.make_async_copy(ref, out, o_sem.at[a])
        cp.start()
        return cp

    own_rows = pl.ds(pl.multiple_of(core * half, half), half)
    mate_rows = pl.ds(pl.multiple_of((1 - core) * half, half), half)

    def core_copy(j, g):
        ks = pl.ds(0, 2) if g == 0 else pl.ds(2, 1)
        return pltpu.make_async_remote_copy(
            core_snd.at[j, ks], core_rcv.at[j, ks], c_send.at[g, j], c_recv.at[g, j],
            device_id=(mate, r, c), device_id_type=MESH)

    def x_copy(j, g):
        ks = pl.ds(0, 2) if g == 0 else pl.ds(2, 1)
        return pltpu.make_async_remote_copy(
            x_snd.at[j, ks], x_rcv.at[j, ks], x_send.at[g, j], x_recv.at[g, j],
            device_id=(across, r, c), device_id_type=MESH)

    def t_copy(j, rows):
        return pltpu.make_async_remote_copy(
            terms.at[:, rows, cols_of(j)], terms.at[:, rows, cols_of(j)],
            t_send.at[j], t_recv.at[j], device_id=(mate, r, c), device_id_type=MESH)

    def split(j, k, p):
        low, high = p[:half], p[half:]
        keep[j, k] = jnp.where(core == 0, low, high)
        core_snd[j, k] = jnp.where(core == 0, high, low).astype(BF)

    def forward(j, g):
        cols = cols_of(j)
        if g == 0:
            w_copy(j, 0).wait()
            w_copy(j, 1).wait()
            split(j, 0, jnp.dot(tok[...], wg[:, cols], preferred_element_type=jnp.float32))
            split(j, 1, jnp.dot(tok[...], wu[:, cols], preferred_element_type=jnp.float32))
        else:
            w_copy(j, 2).wait()
            split(j, 2, contract_cols(grad[...], wd[cols, :]))
        core_copy(j, g).start()

    def chip_sum(j, g):
        core_copy(j, g).wait_recv()
        for k in ((0, 1), (2,))[g]:
            total = keep[j, k] + core_rcv[j, k].astype(jnp.float32)
            keep[j, k] = total
            x_snd[j, k] = total.astype(BF)
        x_copy(j, g).start()

    def finish(j):
        x_copy(j, 0).wait_recv()
        x_copy(j, 1).wait_recv()
        total = keep[j] + x_rcv[j].astype(jnp.float32)
        for k, v in enumerate(swiglu_terms(total[0], total[1], total[2])):
            terms[k, own_rows, cols_of(j)] = v
        t_copy(j, own_rows).start()

    def input_sums(j):
        t_copy(j, mate_rows).wait_recv()
        cols = cols_of(j)
        gate_term, up_term = terms[1, :, cols], terms[2, :, cols]
        for n in range(4):
            rows = slice(n * zw, (n + 1) * zw)
            y[:, rows] += contract_cols(gate_term, wg[rows, cols]) + contract_cols(up_term, wu[rows, cols])

    def tok_step(s, _):
        forward(s, 0)
        pl.when(s >= 1)(lambda: chip_sum(s - 1, 0))
        return 0

    def step(s, _):
        pl.when(s < n_chunk)(lambda: forward(s, 1))
        pl.when((s >= 1) & (s < n_chunk + 1))(lambda: chip_sum(s - 1, 1))
        pl.when((s >= 2) & (s < n_chunk + 2))(lambda: finish(s - 2))
        pl.when(s >= 3)(lambda: input_sums(s - 3))
        return 0

    out_copies = [take(0, tok, tok_out)]
    lax.fori_loop(0, n_chunk, tok_step, 0)
    chip_sum(n_chunk - 1, 0)
    out_copies.append(take(1, grad, grad_out))
    lax.fori_loop(0, n_chunk + 3, step, 0)
    terms_copy = pltpu.make_async_copy(terms, terms_out, o_sem.at[2])
    terms_copy.start()

    def y_copy(o):
        return pltpu.make_async_remote_copy(
            y_snd.at[o], y_rcv.at[o], y_send.at[o], y_recv.at[o],
            device_id=(d, 1 - r, c), device_id_type=MESH)

    def z_copy(o):
        return pltpu.make_async_remote_copy(
            z_snd.at[o], z_rcv.at[o], z_send.at[o], z_recv.at[o],
            device_id=(d, r, lax.rem(c + o, 4)), device_id_type=MESH)

    row_own = pl.ds(pl.multiple_of(r * half, half), half)
    row_other = pl.ds(pl.multiple_of((1 - r) * half, half), half)

    def z_cols(o):
        return pl.ds(pl.multiple_of(lax.rem(c + o, 4) * zw, zw), zw)

    for o in (2, 1, 3, 0):
        y_snd[o] = y[row_other, z_cols(o)].astype(BF)
        y_copy(o).start()
    for o in (2, 1, 3):
        y_copy(o).wait_recv()
        z_snd[o] = (y[row_own, z_cols(o)] + y_rcv[o].astype(jnp.float32)).astype(BF)
        z_copy(o).start()
    y_copy(0).wait_recv()
    acc = y[row_own, z_cols(0)] + y_rcv[0].astype(jnp.float32)
    for o in (1, 3, 2):
        z_copy(o).wait_recv()
        acc = acc + z_rcv[o].astype(jnp.float32)
    acc = acc.astype(BF)
    stacked = jnp.concatenate([acc[:, g * 128:(g + 1) * 128] for g in range(zw // 128)], axis=0)
    owners = jnp.dot(sel_owner[...], stacked, preferred_element_type=jnp.float32).astype(BF)
    f_snd[...] = owners.reshape(f_snd.shape)

    me16 = d * 4 + c

    def f_copy(o):
        to = lax.rem(me16 + o, 16)
        return pltpu.make_async_remote_copy(
            f_snd.at[to], f_rcv.at[me16], f_send.at[o], f_recv.at[o],
            device_id=(lax.div(to, 4), r, lax.rem(to, 4)), device_id_type=MESH)

    for o in range(1, 16):
        f_copy(o).start()
    f_own = pltpu.make_async_copy(f_snd.at[me16], f_rcv.at[me16], f_sem)
    f_own.start()
    f_own.wait()
    for o in range(1, 16):
        frm = lax.rem(me16 + 16 - o, 16)
        pltpu.make_async_remote_copy(
            f_snd.at[0], f_rcv.at[frm], f_send.at[o], f_recv.at[o],
            device_id=(mate, r, c), device_id_type=MESH).wait_recv()
    ig_out[...] = f_rcv[...]

    for cp in a_copies:
        cp.wait_send()

    def drain(j, _):
        for g in range(2):
            core_copy(j, g).wait_send()
            x_copy(j, g).wait_send()
        t_copy(j, own_rows).wait_send()
        return 0

    lax.fori_loop(0, n_chunk, drain, 0)
    for o in range(4):
        y_copy(o).wait_send()
    for o in range(1, 4):
        z_copy(o).wait_send()
    for o in range(1, 16):
        f_copy(o).wait_send()
    for cp in out_copies:
        cp.wait()
    terms_copy.wait()


def grads_kernel(own, groups, tok, grad, hidden, gate_term, up_term, ig, ig_out, gate_grad, up_grad, down_grad, wide, line):
    def assemble():
        wide[...] = ig[...].astype(jnp.float32)
        for n in range(ig.shape[0]):
            for g in range(groups):
                at = (n * groups + g) * 128
                line[0:own, at:at + 128] = wide[n, g * own:(g + 1) * own, :]
        ig_out[...] = line[0:own, :].astype(BF)

    pl.when(pl.program_id(0) == 0)(assemble)
    gate_grad[...] = contract_rows(tok[...], gate_term[0]).astype(BF)
    up_grad[...] = contract_rows(tok[...], up_term[0]).astype(BF)
    down_grad[...] = contract_rows(hidden[0], grad[...]).astype(BF)


def fused(n_depth, n_row, n_col):
    def on_device(tokens, out_grad, gate_weight, up_weight, down_weight):
        blk, model = tokens.shape
        width, units = gate_weight.shape
        own = blk // n_col
        n_tok = n_depth * n_row * blk
        cuts, part = 4, width // 4
        n_chunk = units // CHUNK
        half = n_tok // 2
        zw = width // n_col
        groups = zw // 128
        sel = jnp.asarray(order_tokens(n_depth, n_row, n_col, own, cuts), BF)
        sel_owner = jnp.asarray(order_owners(n_depth, n_col, own, groups), BF)
        sel_owner = sel_owner.reshape(n_depth * n_col * 16, -1)
        vmem, hbm = pl.BlockSpec(memory_space=pltpu.VMEM), pl.BlockSpec(memory_space=pl.ANY)
        dma = pltpu.SemaphoreType.DMA
        tok, grad, terms, ig = pl.pallas_call(
            functools.partial(chain_kernel, n_chunk),
            out_shape=(
                jax.ShapeDtypeStruct((n_tok, width), BF),
                jax.ShapeDtypeStruct((n_tok, width), BF),
                jax.ShapeDtypeStruct((3, n_tok, units), BF),
                jax.ShapeDtypeStruct((16, 16, 128), BF),
            ),
            in_specs=[vmem, vmem, hbm, hbm, hbm, vmem, vmem],
            out_specs=(hbm, hbm, hbm, vmem),
            scratch_shapes=[
                pltpu.VMEM((2, n_depth, cuts * blk, part), BF),
                pltpu.VMEM((cuts * blk, part), jnp.float32),
                pltpu.VMEM((width, units), BF),
                pltpu.VMEM((width, units), BF),
                pltpu.VMEM((units, width), BF),
                pltpu.VMEM((2, n_depth * n_row * cuts * blk, part), BF),
                pltpu.VMEM((n_tok, width), BF),
                pltpu.VMEM((n_tok, width), BF),
                pltpu.VMEM((n_chunk, 3, half, CHUNK), jnp.float32),
                pltpu.VMEM((n_chunk, 3, half, CHUNK), BF),
                pltpu.VMEM((n_chunk, 3, half, CHUNK), BF),
                pltpu.VMEM((n_chunk, 3, half, CHUNK), BF),
                pltpu.VMEM((n_chunk, 3, half, CHUNK), BF),
                pltpu.VMEM((3, n_tok, units), BF),
                pltpu.VMEM((n_tok, width), jnp.float32),
                pltpu.VMEM((4, half, zw), BF),
                pltpu.VMEM((4, half, zw), BF),
                pltpu.VMEM((4, half, zw), BF),
                pltpu.VMEM((4, half, zw), BF),
                pltpu.VMEM((16, 16, 128), BF),
                pltpu.VMEM((16, 16, 128), BF),
                dma((3, n_chunk)),
                dma((2, 8)), dma((2, 8)), dma((2,)),
                dma((2, n_chunk)), dma((2, n_chunk)),
                dma((2, n_chunk)), dma((2, n_chunk)),
                dma((n_chunk,)), dma((n_chunk,)),
                dma((4,)), dma((4,)),
                dma((4,)), dma((4,)),
                dma((16,)), dma((16,)), dma,
                dma((3,)),
            ],
            compiler_params=pltpu.CompilerParams(
                collective_id=0, has_side_effects=True, vmem_limit_bytes=56 * 1024 * 1024
            ),
            cost_estimate=pl.CostEstimate(
                flops=10 * n_tok * width * units, bytes_accessed=6 * width * units, transcendentals=n_tok * units
            ),
        )(tokens, out_grad, gate_weight, up_weight, down_weight, sel, sel_owner)
        rows = 256
        full = lambda *shape: pl.BlockSpec(shape, lambda i: (0,) * len(shape))
        by_rows = pl.BlockSpec((rows, width), lambda i: (i, 0))
        return pl.pallas_call(
            functools.partial(grads_kernel, own, groups),
            grid=(width // rows,),
            out_shape=(
                jax.ShapeDtypeStruct((own, model), BF),
                jax.ShapeDtypeStruct((width, units), BF),
                jax.ShapeDtypeStruct((width, units), BF),
                jax.ShapeDtypeStruct((units, width), BF),
            ),
            in_specs=[
                pl.BlockSpec((n_tok, rows), lambda i: (0, i)),
                full(n_tok, width),
                pl.BlockSpec((1, n_tok, rows), lambda i: (0, 0, i)),
                pl.BlockSpec((1, n_tok, units), lambda i: (1, 0, 0)),
                pl.BlockSpec((1, n_tok, units), lambda i: (2, 0, 0)),
                full(16, 16, 128),
            ],
            out_specs=(full(own, model), by_rows, by_rows, by_rows),
            scratch_shapes=[pltpu.VMEM((16, 16, 128), jnp.float32), pltpu.VMEM((8, model), jnp.float32)],
            compiler_params=pltpu.CompilerParams(vmem_limit_bytes=48 * 1024 * 1024),
        )(tok, grad, terms, terms, terms, ig)

    return on_device


def solution(mesh):
    sizes = mesh.shape
    shape = (sizes["depth"], sizes["row"], sizes["col"])
    on_device = fused(*shape) if shape == (4, 2, 4) else weight_stationary(*shape)
    return jax.shard_map(
        on_device,
        mesh=mesh,
        in_specs=(
            P(("depth", "row"), None),
            P(("depth", "row"), None),
            P("depth", ("row", "col")),
            P("depth", ("row", "col")),
            P(("row", "col"), "depth"),
        ),
        out_specs=(
            P(("depth", "row", "col"), None),
            P("depth", ("row", "col")),
            P("depth", ("row", "col")),
            P(("row", "col"), "depth"),
        ),
        check_vma=False,
    )
```

```python
import functools

import jax
import jax.numpy as jnp
import numpy as np
from jax import lax
from jax.experimental import pallas as pl
from jax.experimental.pallas import tpu as pltpu
from jax.sharding import PartitionSpec as P


def contract_rows(left, right):
    return lax.dot_general(
        left, right, (((0,), (0,)), ((), ())), preferred_element_type=jnp.float32
    )


def contract_cols(left, right):
    return lax.dot_general(
        left, right, (((1,), (1,)), ((), ())), preferred_element_type=jnp.float32
    )


def swiglu_terms(gate, up, hidden_grad):
    sig = jax.nn.sigmoid(gate)
    act = gate * sig
    hidden = (act * up).astype(jnp.bfloat16)
    gate_term = (hidden_grad * up * sig * (1.0 + gate * (1.0 - sig))).astype(jnp.bfloat16)
    up_term = (hidden_grad * act).astype(jnp.bfloat16)
    return (hidden, gate_term, up_term)


def weight_stationary(n_depth, n_row, n_col):
    def on_device(tokens, out_grad, gate_weight, up_weight, down_weight):
        blk = tokens.shape[0]
        both = jnp.stack([tokens, out_grad])
        both = lax.all_to_all(both, "depth", split_axis=2, concat_axis=1, tiled=True)
        both = lax.all_gather(both, "row", axis=1, tiled=True)
        tok, grad = both[0], both[1]
        partial = jnp.stack(
            [
                jnp.dot(tok, gate_weight, preferred_element_type=jnp.float32),
                jnp.dot(tok, up_weight, preferred_element_type=jnp.float32),
                contract_cols(grad, down_weight),
            ]
        )
        sums = lax.psum_scatter(partial, "depth", scatter_dimension=1, tiled=True)
        terms = jnp.stack(swiglu_terms(sums[0], sums[1], sums[2]))
        hidden, gate_term, up_term = lax.all_gather(terms, "depth", axis=1, tiled=True)
        partial_in = contract_cols(gate_term, gate_weight) + contract_cols(up_term, up_weight)
        width = partial_in.shape[1]
        own = blk // n_col
        partial_in = partial_in.reshape(n_row, n_depth, n_col, own, width)
        partial_in = partial_in.transpose(0, 2, 1, 3, 4).reshape(-1, width)
        input_grad = lax.psum_scatter(
            partial_in, ("row", "col"), scatter_dimension=0, tiled=True
        ).astype(jnp.bfloat16)
        input_grad = lax.all_to_all(
            input_grad, "depth", split_axis=0, concat_axis=1, tiled=True
        )
        return (
            input_grad,
            contract_rows(tok, gate_term).astype(jnp.bfloat16),
            contract_rows(tok, up_term).astype(jnp.bfloat16),
            contract_rows(hidden, grad).astype(jnp.bfloat16),
        )

    return on_device


MESH = pl.DeviceIdType.MESH
CHUNK = 512
BF = jnp.bfloat16


def order_tokens(n_depth, n_row, n_col, own, cuts):
    blk = n_col * own
    rows = n_depth * n_row * blk
    out = np.zeros((cuts * rows, cuts * rows), np.float32)
    for cut in range(cuts):
        for r in range(n_row):
            for c in range(n_col):
                for d in range(n_depth):
                    for t in range(own):
                        to = ((r * n_col + c) * n_depth + d) * own + t
                        out[cut * rows + to, ((d * n_row + r) * cuts + cut) * blk + c * own + t] = 1.0
    return out


def order_owners(n_depth, n_col, own, groups):
    out = np.zeros((n_depth * n_col * 16, groups * n_col * n_depth * own), np.float32)
    for d in range(n_depth):
        for c in range(n_col):
            for g in range(groups):
                for t in range(own):
                    out[(d * n_col + c) * 16 + g * own + t, ((g * n_col + c) * n_depth + d) * own + t] = 1.0
    return out


def chain_kernel(
    n_chunk,
    tok_in, grad_in, wg_hbm, wu_hbm, wd_hbm, sel, sel_owner,
    tok_out, grad_out, terms_out, ig_out,
    pk, stage, wg, wu, wd, arrived, tok, grad, keep, core_snd, core_rcv, x_snd, x_rcv, terms, y,
    y_snd, y_rcv, z_snd, z_rcv, f_snd, f_rcv,
    w_sem, a_send, a_recv, a_sem, c_send, c_recv, x_send, x_recv, t_send, t_recv,
    y_send, y_recv, z_send, z_recv, f_send, f_recv, f_sem, o_sem,
):
    d, r, c = lax.axis_index("depth"), lax.axis_index("row"), lax.axis_index("col")
    core, chip = lax.rem(d, 2), lax.div(d, 2)
    mate = d + 1 - 2 * core
    across = d + 2 - 4 * chip
    width = wg.shape[0]
    cw = CHUNK
    half = tok.shape[0] // 2
    zw = width // 4

    def cols_of(j):
        return pl.ds(pl.multiple_of(j * cw, cw), cw)

    def w_copy(j, k):
        cols = cols_of(j)
        at = (cols, slice(None)) if k == 2 else (slice(None), cols)
        src, dst = ((wg_hbm, wg), (wu_hbm, wu), (wd_hbm, wd))[k]
        return pltpu.make_async_copy(src.at[at], dst.at[at], w_sem.at[k, j])

    for k in ((0, 1), (2,)):
        for j in range(n_chunk):
            for i in k:
                w_copy(j, i).start()

    barrier = pltpu.get_barrier_semaphore()
    me8 = d * 2 + r
    for o in range(1, 8):
        to = lax.rem(me8 + o, 8)
        pl.semaphore_signal(barrier, inc=1, device_id=(lax.div(to, 2), lax.rem(to, 2), c), device_id_type=MESH)
    for oc in range(1, 4):
        for od in range(4):
            pl.semaphore_signal(barrier, inc=1, device_id=(lax.rem(d + od, 4), r, lax.rem(c + oc, 4)), device_id_type=MESH)
    blk, part = pk.shape[2:]
    cuts = width // part
    own_blk = blk // cuts
    for a, ref in ((0, tok_in), (1, grad_in)):
        for q in range(4):
            for h in range(cuts):
                at = q * width + h * part
                stage[h * own_blk:(h + 1) * own_blk, :] = ref[:, at:at + part].astype(jnp.float32)
            pk[a, q] = stage[...].astype(BF)
    y[...] = jnp.zeros_like(y)
    pl.semaphore_wait(barrier, 19)

    mine = pl.ds(pl.multiple_of(me8 * blk, blk), blk)
    a_copies = []
    for a in range(2):
        for o in range(1, 8):
            to = lax.rem(me8 + o, 8)
            to_d, to_r = lax.div(to, 2), lax.rem(to, 2)
            a_copies.append(pltpu.make_async_remote_copy(
                pk.at[a, to_d], arrived.at[a, mine, :], a_send.at[a, o], a_recv.at[a, o],
                device_id=(to_d, to_r, c), device_id_type=MESH))
    for cp in a_copies:
        cp.start()
    own_copies = [pltpu.make_async_copy(pk.at[a, d], arrived.at[a, mine, :], a_sem.at[a]) for a in range(2)]
    for cp in own_copies:
        cp.start()
    n_tok = tok.shape[0]

    def take(a, ref, out):
        own_copies[a].wait()
        for o in range(1, 8):
            frm = lax.rem(me8 + 8 - o, 8)
            rows = pl.ds(pl.multiple_of(frm * blk, blk), blk)
            pltpu.make_async_remote_copy(
                pk.at[a, 0], arrived.at[a, rows, :], a_send.at[a, o], a_recv.at[a, o],
                device_id=(mate, r, c), device_id_type=MESH).wait_recv()
        for h in range(cuts):
            ref[:, h * part:(h + 1) * part] = jnp.dot(
                sel[h * n_tok:(h + 1) * n_tok, :], arrived[a], preferred_element_type=jnp.float32
            ).astype(BF)
        cp = pltpu.make_async_copy(ref, out, o_sem.at[a])
        cp.start()
        return cp

    own_rows = pl.ds(pl.multiple_of(core * half, half), half)
    mate_rows = pl.ds(pl.multiple_of((1 - core) * half, half), half)

    def core_copy(j, g):
        ks = pl.ds(0, 2) if g == 0 else pl.ds(2, 1)
        return pltpu.make_async_remote_copy(
            core_snd.at[j, ks], core_rcv.at[j, ks], c_send.at[g, j], c_recv.at[g, j],
            device_id=(mate, r, c), device_id_type=MESH)

    def x_copy(j, g):
        ks = pl.ds(0, 2) if g == 0 else pl.ds(2, 1)
        return pltpu.make_async_remote_copy(
            x_snd.at[j, ks], x_rcv.at[j, ks], x_send.at[g, j], x_recv.at[g, j],
            device_id=(across, r, c), device_id_type=MESH)

    def t_copy(j, rows):
        return pltpu.make_async_remote_copy(
            terms.at[:, rows, cols_of(j)], terms.at[:, rows, cols_of(j)],
            t_send.at[j], t_recv.at[j], device_id=(mate, r, c), device_id_type=MESH)

    def split(j, k, p):
        low, high = p[:half], p[half:]
        keep[j, k] = jnp.where(core == 0, low, high)
        core_snd[j, k] = jnp.where(core == 0, high, low).astype(BF)

    def forward(j, g):
        cols = cols_of(j)
        if g == 0:
            w_copy(j, 0).wait()
            w_copy(j, 1).wait()
            split(j, 0, jnp.dot(tok[...], wg[:, cols], preferred_element_type=jnp.float32))
            split(j, 1, jnp.dot(tok[...], wu[:, cols], preferred_element_type=jnp.float32))
        else:
            w_copy(j, 2).wait()
            split(j, 2, contract_cols(grad[...], wd[cols, :]))
        core_copy(j, g).start()

    def chip_sum(j, g):
        core_copy(j, g).wait_recv()
        for k in ((0, 1), (2,))[g]:
            total = keep[j, k] + core_rcv[j, k].astype(jnp.float32)
            keep[j, k] = total
            x_snd[j, k] = total.astype(BF)
        x_copy(j, g).start()

    def finish(j):
        x_copy(j, 0).wait_recv()
        x_copy(j, 1).wait_recv()
        total = keep[j] + x_rcv[j].astype(jnp.float32)
        for k, v in enumerate(swiglu_terms(total[0], total[1], total[2])):
            terms[k, own_rows, cols_of(j)] = v
        t_copy(j, own_rows).start()

    def add_input(j, at):
        cols = cols_of(j)
        y[:, at] += contract_cols(terms[1, :, cols], wg[at, cols]) + contract_cols(terms[2, :, cols], wu[at, cols])

    def input_sums(j):
        t_copy(j, mate_rows).wait_recv()
        for n in range(4):
            add_input(j, slice(n * zw, (n + 1) * zw))

    def tok_step(s, _):
        forward(s, 0)
        pl.when(s >= 1)(lambda: chip_sum(s - 1, 0))
        return 0

    def step(s, _):
        pl.when(s < n_chunk)(lambda: forward(s, 1))
        pl.when((s >= 1) & (s < n_chunk + 1))(lambda: chip_sum(s - 1, 1))
        pl.when(s >= 2)(lambda: finish(s - 2))
        pl.when(s >= 3)(lambda: input_sums(s - 3))
        return 0

    out_copies = [take(0, tok, tok_out)]
    lax.fori_loop(0, n_chunk, tok_step, 0)
    chip_sum(n_chunk - 1, 0)
    out_copies.append(take(1, grad, grad_out))
    lax.fori_loop(0, n_chunk + 2, step, 0)
    t_copy(n_chunk - 1, mate_rows).wait_recv()
    terms_copy = pltpu.make_async_copy(terms, terms_out, o_sem.at[2])
    terms_copy.start()

    def y_copy(o):
        return pltpu.make_async_remote_copy(
            y_snd.at[o], y_rcv.at[o], y_send.at[o], y_recv.at[o],
            device_id=(d, 1 - r, c), device_id_type=MESH)

    def z_copy(o):
        return pltpu.make_async_remote_copy(
            z_snd.at[o], z_rcv.at[o], z_send.at[o], z_recv.at[o],
            device_id=(d, r, lax.rem(c + o, 4)), device_id_type=MESH)

    row_own = pl.ds(pl.multiple_of(r * half, half), half)
    row_other = pl.ds(pl.multiple_of((1 - r) * half, half), half)

    def z_cols(o):
        return pl.ds(pl.multiple_of(lax.rem(c + o, 4) * zw, zw), zw)

    for o in (2, 1, 3, 0):
        add_input(n_chunk - 1, z_cols(o))
        y_snd[o] = y[row_other, z_cols(o)].astype(BF)
        y_copy(o).start()
    for o in (2, 1, 3):
        y_copy(o).wait_recv()
        z_snd[o] = (y[row_own, z_cols(o)] + y_rcv[o].astype(jnp.float32)).astype(BF)
        z_copy(o).start()
    y_copy(0).wait_recv()
    acc = y[row_own, z_cols(0)] + y_rcv[0].astype(jnp.float32)
    for o in (1, 3, 2):
        z_copy(o).wait_recv()
        acc = acc + z_rcv[o].astype(jnp.float32)
    acc = acc.astype(BF)
    stacked = jnp.concatenate([acc[:, g * 128:(g + 1) * 128] for g in range(zw // 128)], axis=0)
    owners = jnp.dot(sel_owner[...], stacked, preferred_element_type=jnp.float32).astype(BF)
    f_snd[...] = owners.reshape(f_snd.shape)

    me16 = d * 4 + c

    def f_copy(o):
        to = lax.rem(me16 + o, 16)
        return pltpu.make_async_remote_copy(
            f_snd.at[to], f_rcv.at[me16], f_send.at[o], f_recv.at[o],
            device_id=(lax.div(to, 4), r, lax.rem(to, 4)), device_id_type=MESH)

    for o in range(1, 16):
        f_copy(o).start()
    f_own = pltpu.make_async_copy(f_snd.at[me16], f_rcv.at[me16], f_sem)
    f_own.start()
    f_own.wait()
    for o in range(1, 16):
        frm = lax.rem(me16 + 16 - o, 16)
        pltpu.make_async_remote_copy(
            f_snd.at[0], f_rcv.at[frm], f_send.at[o], f_recv.at[o],
            device_id=(mate, r, c), device_id_type=MESH).wait_recv()
    ig_out[...] = f_rcv[...]

    for cp in a_copies:
        cp.wait_send()

    def drain(j, _):
        for g in range(2):
            core_copy(j, g).wait_send()
            x_copy(j, g).wait_send()
        t_copy(j, own_rows).wait_send()
        return 0

    lax.fori_loop(0, n_chunk, drain, 0)
    for o in range(4):
        y_copy(o).wait_send()
    for o in range(1, 4):
        z_copy(o).wait_send()
    for o in range(1, 16):
        f_copy(o).wait_send()
    for cp in out_copies:
        cp.wait()
    terms_copy.wait()


def grads_kernel(own, groups, tok, grad, hidden, gate_term, up_term, ig, ig_out, gate_grad, up_grad, down_grad, wide, line):
    def assemble():
        wide[...] = ig[...].astype(jnp.float32)
        for n in range(ig.shape[0]):
            for g in range(groups):
                at = (n * groups + g) * 128
                line[0:own, at:at + 128] = wide[n, g * own:(g + 1) * own, :]
        ig_out[...] = line[0:own, :].astype(BF)

    pl.when(pl.program_id(0) == 0)(assemble)
    gate_grad[...] = contract_rows(tok[...], gate_term[0]).astype(BF)
    up_grad[...] = contract_rows(tok[...], up_term[0]).astype(BF)
    down_grad[...] = contract_rows(hidden[0], grad[...]).astype(BF)


def fused(n_depth, n_row, n_col):
    def on_device(tokens, out_grad, gate_weight, up_weight, down_weight):
        blk, model = tokens.shape
        width, units = gate_weight.shape
        own = blk // n_col
        n_tok = n_depth * n_row * blk
        cuts, part = 4, width // 4
        n_chunk = units // CHUNK
        half = n_tok // 2
        zw = width // n_col
        groups = zw // 128
        sel = jnp.asarray(order_tokens(n_depth, n_row, n_col, own, cuts), BF)
        sel_owner = jnp.asarray(order_owners(n_depth, n_col, own, groups), BF)
        sel_owner = sel_owner.reshape(n_depth * n_col * 16, -1)
        vmem, hbm = pl.BlockSpec(memory_space=pltpu.VMEM), pl.BlockSpec(memory_space=pl.ANY)
        dma = pltpu.SemaphoreType.DMA
        tok, grad, terms, ig = pl.pallas_call(
            functools.partial(chain_kernel, n_chunk),
            out_shape=(
                jax.ShapeDtypeStruct((n_tok, width), BF),
                jax.ShapeDtypeStruct((n_tok, width), BF),
                jax.ShapeDtypeStruct((3, n_tok, units), BF),
                jax.ShapeDtypeStruct((16, 16, 128), BF),
            ),
            in_specs=[vmem, vmem, hbm, hbm, hbm, vmem, vmem],
            out_specs=(hbm, hbm, hbm, vmem),
            scratch_shapes=[
                pltpu.VMEM((2, n_depth, cuts * blk, part), BF),
                pltpu.VMEM((cuts * blk, part), jnp.float32),
                pltpu.VMEM((width, units), BF),
                pltpu.VMEM((width, units), BF),
                pltpu.VMEM((units, width), BF),
                pltpu.VMEM((2, n_depth * n_row * cuts * blk, part), BF),
                pltpu.VMEM((n_tok, width), BF),
                pltpu.VMEM((n_tok, width), BF),
                pltpu.VMEM((n_chunk, 3, half, CHUNK), jnp.float32),
                pltpu.VMEM((n_chunk, 3, half, CHUNK), BF),
                pltpu.VMEM((n_chunk, 3, half, CHUNK), BF),
                pltpu.VMEM((n_chunk, 3, half, CHUNK), BF),
                pltpu.VMEM((n_chunk, 3, half, CHUNK), BF),
                pltpu.VMEM((3, n_tok, units), BF),
                pltpu.VMEM((n_tok, width), jnp.float32),
                pltpu.VMEM((4, half, zw), BF),
                pltpu.VMEM((4, half, zw), BF),
                pltpu.VMEM((4, half, zw), BF),
                pltpu.VMEM((4, half, zw), BF),
                pltpu.VMEM((16, 16, 128), BF),
                pltpu.VMEM((16, 16, 128), BF),
                dma((3, n_chunk)),
                dma((2, 8)), dma((2, 8)), dma((2,)),
                dma((2, n_chunk)), dma((2, n_chunk)),
                dma((2, n_chunk)), dma((2, n_chunk)),
                dma((n_chunk,)), dma((n_chunk,)),
                dma((4,)), dma((4,)),
                dma((4,)), dma((4,)),
                dma((16,)), dma((16,)), dma,
                dma((3,)),
            ],
            compiler_params=pltpu.CompilerParams(
                collective_id=0, has_side_effects=True, vmem_limit_bytes=56 * 1024 * 1024
            ),
            cost_estimate=pl.CostEstimate(
                flops=10 * n_tok * width * units, bytes_accessed=6 * width * units, transcendentals=n_tok * units
            ),
        )(tokens, out_grad, gate_weight, up_weight, down_weight, sel, sel_owner)
        rows = 256
        full = lambda *shape: pl.BlockSpec(shape, lambda i: (0,) * len(shape))
        by_rows = pl.BlockSpec((rows, width), lambda i: (i, 0))
        return pl.pallas_call(
            functools.partial(grads_kernel, own, groups),
            grid=(width // rows,),
            out_shape=(
                jax.ShapeDtypeStruct((own, model), BF),
                jax.ShapeDtypeStruct((width, units), BF),
                jax.ShapeDtypeStruct((width, units), BF),
                jax.ShapeDtypeStruct((units, width), BF),
            ),
            in_specs=[
                pl.BlockSpec((n_tok, rows), lambda i: (0, i)),
                full(n_tok, width),
                pl.BlockSpec((1, n_tok, rows), lambda i: (0, 0, i)),
                pl.BlockSpec((1, n_tok, units), lambda i: (1, 0, 0)),
                pl.BlockSpec((1, n_tok, units), lambda i: (2, 0, 0)),
                full(16, 16, 128),
            ],
            out_specs=(full(own, model), by_rows, by_rows, by_rows),
            scratch_shapes=[pltpu.VMEM((16, 16, 128), jnp.float32), pltpu.VMEM((8, model), jnp.float32)],
            compiler_params=pltpu.CompilerParams(vmem_limit_bytes=62 * 1024 * 1024),
        )(tok, grad, terms, terms, terms, ig)

    return on_device


def solution(mesh):
    sizes = mesh.shape
    shape = (sizes["depth"], sizes["row"], sizes["col"])
    on_device = fused(*shape) if shape == (4, 2, 4) else weight_stationary(*shape)
    return jax.shard_map(
        on_device,
        mesh=mesh,
        in_specs=(
            P(("depth", "row"), None),
            P(("depth", "row"), None),
            P("depth", ("row", "col")),
            P("depth", ("row", "col")),
            P(("row", "col"), "depth"),
        ),
        out_specs=(
            P(("depth", "row", "col"), None),
            P("depth", ("row", "col")),
            P("depth", ("row", "col")),
            P(("row", "col"), "depth"),
        ),
        check_vma=False,
    )
```

```python
import functools

import jax
import jax.numpy as jnp
import numpy as np
from jax import lax
from jax.experimental import pallas as pl
from jax.experimental.pallas import tpu as pltpu
from jax.sharding import PartitionSpec as P


def contract_rows(left, right):
    return lax.dot_general(
        left, right, (((0,), (0,)), ((), ())), preferred_element_type=jnp.float32
    )


def contract_cols(left, right):
    return lax.dot_general(
        left, right, (((1,), (1,)), ((), ())), preferred_element_type=jnp.float32
    )


def swiglu_terms(gate, up, hidden_grad):
    sig = jax.nn.sigmoid(gate)
    act = gate * sig
    hidden = (act * up).astype(jnp.bfloat16)
    gate_term = (hidden_grad * up * sig * (1.0 + gate * (1.0 - sig))).astype(jnp.bfloat16)
    up_term = (hidden_grad * act).astype(jnp.bfloat16)
    return (hidden, gate_term, up_term)


def weight_stationary(n_depth, n_row, n_col):
    def on_device(tokens, out_grad, gate_weight, up_weight, down_weight):
        blk = tokens.shape[0]
        both = jnp.stack([tokens, out_grad])
        both = lax.all_to_all(both, "depth", split_axis=2, concat_axis=1, tiled=True)
        both = lax.all_gather(both, "row", axis=1, tiled=True)
        tok, grad = both[0], both[1]
        partial = jnp.stack(
            [
                jnp.dot(tok, gate_weight, preferred_element_type=jnp.float32),
                jnp.dot(tok, up_weight, preferred_element_type=jnp.float32),
                contract_cols(grad, down_weight),
            ]
        )
        sums = lax.psum_scatter(partial, "depth", scatter_dimension=1, tiled=True)
        terms = jnp.stack(swiglu_terms(sums[0], sums[1], sums[2]))
        hidden, gate_term, up_term = lax.all_gather(terms, "depth", axis=1, tiled=True)
        partial_in = contract_cols(gate_term, gate_weight) + contract_cols(up_term, up_weight)
        width = partial_in.shape[1]
        own = blk // n_col
        partial_in = partial_in.reshape(n_row, n_depth, n_col, own, width)
        partial_in = partial_in.transpose(0, 2, 1, 3, 4).reshape(-1, width)
        input_grad = lax.psum_scatter(
            partial_in, ("row", "col"), scatter_dimension=0, tiled=True
        ).astype(jnp.bfloat16)
        input_grad = lax.all_to_all(
            input_grad, "depth", split_axis=0, concat_axis=1, tiled=True
        )
        return (
            input_grad,
            contract_rows(tok, gate_term).astype(jnp.bfloat16),
            contract_rows(tok, up_term).astype(jnp.bfloat16),
            contract_rows(hidden, grad).astype(jnp.bfloat16),
        )

    return on_device


MESH = pl.DeviceIdType.MESH
CHUNK = 512
BF = jnp.bfloat16


def order_tokens(n_depth, n_row, n_col, own, cuts):
    blk = n_col * own
    rows = n_depth * n_row * blk
    out = np.zeros((cuts * rows, cuts * rows), np.float32)
    for cut in range(cuts):
        for r in range(n_row):
            for c in range(n_col):
                for d in range(n_depth):
                    for t in range(own):
                        to = ((r * n_col + c) * n_depth + d) * own + t
                        out[cut * rows + to, ((d * n_row + r) * cuts + cut) * blk + c * own + t] = 1.0
    return out


def order_owners(n_depth, n_col, own, groups):
    out = np.zeros((n_depth * n_col * 16, groups * n_col * n_depth * own), np.float32)
    for d in range(n_depth):
        for c in range(n_col):
            for g in range(groups):
                for t in range(own):
                    out[(d * n_col + c) * 16 + g * own + t, ((g * n_col + c) * n_depth + d) * own + t] = 1.0
    return out


def chain_kernel(
    n_chunk,
    tok_in, grad_in, wg_hbm, wu_hbm, wd_hbm, sel, sel_owner,
    tok_out, grad_out, terms_out, ig_out,
    pk, stage, wg, wu, wd, arrived, tok, grad, keep, core_snd, core_rcv, x_snd, x_rcv, terms, y,
    y_snd, y_rcv, z_snd, z_rcv, f_snd, f_rcv,
    w_sem, a_send, a_recv, a_sem, c_send, c_recv, x_send, x_recv, t_send, t_recv,
    y_send, y_recv, z_send, z_recv, f_send, f_recv, f_sem, o_sem,
):
    d, r, c = lax.axis_index("depth"), lax.axis_index("row"), lax.axis_index("col")
    core, chip = lax.rem(d, 2), lax.div(d, 2)
    mate = d + 1 - 2 * core
    across = d + 2 - 4 * chip
    width = wg.shape[0]
    cw = CHUNK
    half = tok.shape[0] // 2
    zw = width // 4

    def cols_of(j):
        return pl.ds(pl.multiple_of(j * cw, cw), cw)

    def w_copy(j, k):
        cols = cols_of(j)
        at = (cols, slice(None)) if k == 2 else (slice(None), cols)
        src, dst = ((wg_hbm, wg), (wu_hbm, wu), (wd_hbm, wd))[k]
        return pltpu.make_async_copy(src.at[at], dst.at[at], w_sem.at[k, j])

    for k in ((0, 1), (2,)):
        for j in range(n_chunk):
            for i in k:
                w_copy(j, i).start()

    barrier = pltpu.get_barrier_semaphore()
    me8 = d * 2 + r
    for o in range(1, 8):
        to = lax.rem(me8 + o, 8)
        pl.semaphore_signal(barrier, inc=1, device_id=(lax.div(to, 2), lax.rem(to, 2), c), device_id_type=MESH)
    for oc in range(1, 4):
        for od in range(4):
            pl.semaphore_signal(barrier, inc=1, device_id=(lax.rem(d + od, 4), r, lax.rem(c + oc, 4)), device_id_type=MESH)
    blk, part = pk.shape[2:]
    cuts = width // part
    own_blk = blk // cuts
    for a, ref in ((0, tok_in), (1, grad_in)):
        for q in range(4):
            for h in range(cuts):
                at = q * width + h * part
                stage[h * own_blk:(h + 1) * own_blk, :] = ref[:, at:at + part].astype(jnp.float32)
            pk[a, q] = stage[...].astype(BF)
    y[...] = jnp.zeros_like(y)
    pl.semaphore_wait(barrier, 19)

    mine = pl.ds(pl.multiple_of(me8 * blk, blk), blk)
    a_copies = []
    for a in range(2):
        for o in range(1, 8):
            to = lax.rem(me8 + o, 8)
            to_d, to_r = lax.div(to, 2), lax.rem(to, 2)
            a_copies.append(pltpu.make_async_remote_copy(
                pk.at[a, to_d], arrived.at[a, mine, :], a_send.at[a, o], a_recv.at[a, o],
                device_id=(to_d, to_r, c), device_id_type=MESH))
    tok_copies, grad_copies = a_copies[:7], a_copies[7:]
    for cp in tok_copies:
        cp.start()
    own_copies = [pltpu.make_async_copy(pk.at[a, d], arrived.at[a, mine, :], a_sem.at[a]) for a in range(2)]
    for cp in own_copies:
        cp.start()
    n_tok = tok.shape[0]

    def take(a, ref, out):
        own_copies[a].wait()
        for o in range(1, 8):
            frm = lax.rem(me8 + 8 - o, 8)
            rows = pl.ds(pl.multiple_of(frm * blk, blk), blk)
            pltpu.make_async_remote_copy(
                pk.at[a, 0], arrived.at[a, rows, :], a_send.at[a, o], a_recv.at[a, o],
                device_id=(mate, r, c), device_id_type=MESH).wait_recv()
        for h in range(cuts):
            ref[:, h * part:(h + 1) * part] = jnp.dot(
                sel[h * n_tok:(h + 1) * n_tok, :], arrived[a], preferred_element_type=jnp.float32
            ).astype(BF)
        cp = pltpu.make_async_copy(ref, out, o_sem.at[a])
        cp.start()
        return cp

    own_rows = pl.ds(pl.multiple_of(core * half, half), half)
    mate_rows = pl.ds(pl.multiple_of((1 - core) * half, half), half)

    def core_copy(j, g):
        ks = pl.ds(0, 2) if g == 0 else pl.ds(2, 1)
        return pltpu.make_async_remote_copy(
            core_snd.at[j, ks], core_rcv.at[j, ks], c_send.at[g, j], c_recv.at[g, j],
            device_id=(mate, r, c), device_id_type=MESH)

    def x_copy(j, g):
        ks = pl.ds(0, 2) if g == 0 else pl.ds(2, 1)
        return pltpu.make_async_remote_copy(
            x_snd.at[j, ks], x_rcv.at[j, ks], x_send.at[g, j], x_recv.at[g, j],
            device_id=(across, r, c), device_id_type=MESH)

    def t_copy(j, rows):
        return pltpu.make_async_remote_copy(
            terms.at[:, rows, cols_of(j)], terms.at[:, rows, cols_of(j)],
            t_send.at[j], t_recv.at[j], device_id=(mate, r, c), device_id_type=MESH)

    def split(j, k, p):
        low, high = p[:half], p[half:]
        keep[j, k] = jnp.where(core == 0, low, high)
        core_snd[j, k] = jnp.where(core == 0, high, low).astype(BF)

    def forward(j, g):
        cols = cols_of(j)
        if g == 0:
            w_copy(j, 0).wait()
            w_copy(j, 1).wait()
            split(j, 0, jnp.dot(tok[...], wg[:, cols], preferred_element_type=jnp.float32))
            split(j, 1, jnp.dot(tok[...], wu[:, cols], preferred_element_type=jnp.float32))
        else:
            w_copy(j, 2).wait()
            split(j, 2, contract_cols(grad[...], wd[cols, :]))
        core_copy(j, g).start()

    def chip_sum(j, g):
        core_copy(j, g).wait_recv()
        for k in ((0, 1), (2,))[g]:
            total = keep[j, k] + core_rcv[j, k].astype(jnp.float32)
            keep[j, k] = total
            x_snd[j, k] = total.astype(BF)
        x_copy(j, g).start()

    def finish(j):
        x_copy(j, 0).wait_recv()
        x_copy(j, 1).wait_recv()
        total = keep[j] + x_rcv[j].astype(jnp.float32)
        for k, v in enumerate(swiglu_terms(total[0], total[1], total[2])):
            terms[k, own_rows, cols_of(j)] = v
        t_copy(j, own_rows).start()

    def add_input(j, at):
        cols = cols_of(j)
        y[:, at] += contract_cols(terms[1, :, cols], wg[at, cols]) + contract_cols(terms[2, :, cols], wu[at, cols])

    def input_sums(j):
        t_copy(j, mate_rows).wait_recv()
        for n in range(4):
            add_input(j, slice(n * zw, (n + 1) * zw))

    def tok_step(s, _):
        forward(s, 0)
        pl.when(s >= 1)(lambda: chip_sum(s - 1, 0))
        return 0

    def step(s, _):
        pl.when(s < n_chunk)(lambda: forward(s, 1))
        pl.when((s >= 1) & (s < n_chunk + 1))(lambda: chip_sum(s - 1, 1))
        pl.when(s >= 2)(lambda: finish(s - 2))
        pl.when(s >= 3)(lambda: input_sums(s - 3))
        return 0

    for cp in tok_copies:
        cp.wait_send()
    for cp in grad_copies:
        cp.start()
    out_copies = [take(0, tok, tok_out)]
    lax.fori_loop(0, n_chunk, tok_step, 0)
    chip_sum(n_chunk - 1, 0)
    out_copies.append(take(1, grad, grad_out))
    lax.fori_loop(0, n_chunk + 2, step, 0)
    t_copy(n_chunk - 1, mate_rows).wait_recv()
    terms_copy = pltpu.make_async_copy(terms, terms_out, o_sem.at[2])
    terms_copy.start()

    def y_copy(o):
        return pltpu.make_async_remote_copy(
            y_snd.at[o], y_rcv.at[o], y_send.at[o], y_recv.at[o],
            device_id=(d, 1 - r, c), device_id_type=MESH)

    def z_copy(o):
        return pltpu.make_async_remote_copy(
            z_snd.at[o], z_rcv.at[o], z_send.at[o], z_recv.at[o],
            device_id=(d, r, lax.rem(c + o, 4)), device_id_type=MESH)

    row_own = pl.ds(pl.multiple_of(r * half, half), half)
    row_other = pl.ds(pl.multiple_of((1 - r) * half, half), half)

    def z_cols(o):
        return pl.ds(pl.multiple_of(lax.rem(c + o, 4) * zw, zw), zw)

    for o in (2, 1, 3, 0):
        add_input(n_chunk - 1, z_cols(o))
        y_snd[o] = y[row_other, z_cols(o)].astype(BF)
        y_copy(o).start()
    for o in (2, 1, 3):
        y_copy(o).wait_recv()
        z_snd[o] = (y[row_own, z_cols(o)] + y_rcv[o].astype(jnp.float32)).astype(BF)
        z_copy(o).start()
    y_copy(0).wait_recv()
    acc = y[row_own, z_cols(0)] + y_rcv[0].astype(jnp.float32)
    for o in (1, 3, 2):
        z_copy(o).wait_recv()
        acc = acc + z_rcv[o].astype(jnp.float32)
    acc = acc.astype(BF)
    stacked = jnp.concatenate([acc[:, g * 128:(g + 1) * 128] for g in range(zw // 128)], axis=0)
    owners = jnp.dot(sel_owner[...], stacked, preferred_element_type=jnp.float32).astype(BF)
    f_snd[...] = owners.reshape(f_snd.shape)

    me16 = d * 4 + c

    def f_copy(o):
        to = lax.rem(me16 + o, 16)
        return pltpu.make_async_remote_copy(
            f_snd.at[to], f_rcv.at[me16], f_send.at[o], f_recv.at[o],
            device_id=(lax.div(to, 4), r, lax.rem(to, 4)), device_id_type=MESH)

    for o in range(1, 16):
        f_copy(o).start()
    f_own = pltpu.make_async_copy(f_snd.at[me16], f_rcv.at[me16], f_sem)
    f_own.start()
    f_own.wait()
    for o in range(1, 16):
        frm = lax.rem(me16 + 16 - o, 16)
        pltpu.make_async_remote_copy(
            f_snd.at[0], f_rcv.at[frm], f_send.at[o], f_recv.at[o],
            device_id=(mate, r, c), device_id_type=MESH).wait_recv()
    ig_out[...] = f_rcv[...]

    for cp in grad_copies:
        cp.wait_send()

    def drain(j, _):
        for g in range(2):
            core_copy(j, g).wait_send()
            x_copy(j, g).wait_send()
        t_copy(j, own_rows).wait_send()
        return 0

    lax.fori_loop(0, n_chunk, drain, 0)
    for o in range(4):
        y_copy(o).wait_send()
    for o in range(1, 4):
        z_copy(o).wait_send()
    for o in range(1, 16):
        f_copy(o).wait_send()
    for cp in out_copies:
        cp.wait()
    terms_copy.wait()


def grads_kernel(own, groups, tok, grad, hidden, gate_term, up_term, ig, ig_out, gate_grad, up_grad, down_grad, wide, line):
    def assemble():
        wide[...] = ig[...].astype(jnp.float32)
        for n in range(ig.shape[0]):
            for g in range(groups):
                at = (n * groups + g) * 128
                line[0:own, at:at + 128] = wide[n, g * own:(g + 1) * own, :]
        ig_out[...] = line[0:own, :].astype(BF)

    pl.when(pl.program_id(0) == 0)(assemble)
    gate_grad[...] = contract_rows(tok[...], gate_term[0]).astype(BF)
    up_grad[...] = contract_rows(tok[...], up_term[0]).astype(BF)
    down_grad[...] = contract_rows(hidden[0], grad[...]).astype(BF)


def fused(n_depth, n_row, n_col):
    def on_device(tokens, out_grad, gate_weight, up_weight, down_weight):
        blk, model = tokens.shape
        width, units = gate_weight.shape
        own = blk // n_col
        n_tok = n_depth * n_row * blk
        cuts, part = 4, width // 4
        n_chunk = units // CHUNK
        half = n_tok // 2
        zw = width // n_col
        groups = zw // 128
        sel = jnp.asarray(order_tokens(n_depth, n_row, n_col, own, cuts), BF)
        sel_owner = jnp.asarray(order_owners(n_depth, n_col, own, groups), BF)
        sel_owner = sel_owner.reshape(n_depth * n_col * 16, -1)
        vmem, hbm = pl.BlockSpec(memory_space=pltpu.VMEM), pl.BlockSpec(memory_space=pl.ANY)
        dma = pltpu.SemaphoreType.DMA
        tok, grad, terms, ig = pl.pallas_call(
            functools.partial(chain_kernel, n_chunk),
            out_shape=(
                jax.ShapeDtypeStruct((n_tok, width), BF),
                jax.ShapeDtypeStruct((n_tok, width), BF),
                jax.ShapeDtypeStruct((3, n_tok, units), BF),
                jax.ShapeDtypeStruct((16, 16, 128), BF),
            ),
            in_specs=[vmem, vmem, hbm, hbm, hbm, vmem, vmem],
            out_specs=(hbm, hbm, hbm, vmem),
            scratch_shapes=[
                pltpu.VMEM((2, n_depth, cuts * blk, part), BF),
                pltpu.VMEM((cuts * blk, part), jnp.float32),
                pltpu.VMEM((width, units), BF),
                pltpu.VMEM((width, units), BF),
                pltpu.VMEM((units, width), BF),
                pltpu.VMEM((2, n_depth * n_row * cuts * blk, part), BF),
                pltpu.VMEM((n_tok, width), BF),
                pltpu.VMEM((n_tok, width), BF),
                pltpu.VMEM((n_chunk, 3, half, CHUNK), jnp.float32),
                pltpu.VMEM((n_chunk, 3, half, CHUNK), BF),
                pltpu.VMEM((n_chunk, 3, half, CHUNK), BF),
                pltpu.VMEM((n_chunk, 3, half, CHUNK), BF),
                pltpu.VMEM((n_chunk, 3, half, CHUNK), BF),
                pltpu.VMEM((3, n_tok, units), BF),
                pltpu.VMEM((n_tok, width), jnp.float32),
                pltpu.VMEM((4, half, zw), BF),
                pltpu.VMEM((4, half, zw), BF),
                pltpu.VMEM((4, half, zw), BF),
                pltpu.VMEM((4, half, zw), BF),
                pltpu.VMEM((16, 16, 128), BF),
                pltpu.VMEM((16, 16, 128), BF),
                dma((3, n_chunk)),
                dma((2, 8)), dma((2, 8)), dma((2,)),
                dma((2, n_chunk)), dma((2, n_chunk)),
                dma((2, n_chunk)), dma((2, n_chunk)),
                dma((n_chunk,)), dma((n_chunk,)),
                dma((4,)), dma((4,)),
                dma((4,)), dma((4,)),
                dma((16,)), dma((16,)), dma,
                dma((3,)),
            ],
            compiler_params=pltpu.CompilerParams(
                collective_id=0, has_side_effects=True, vmem_limit_bytes=56 * 1024 * 1024
            ),
            cost_estimate=pl.CostEstimate(
                flops=10 * n_tok * width * units, bytes_accessed=6 * width * units, transcendentals=n_tok * units
            ),
        )(tokens, out_grad, gate_weight, up_weight, down_weight, sel, sel_owner)
        rows = 256
        full = lambda *shape: pl.BlockSpec(shape, lambda i: (0,) * len(shape))
        by_rows = pl.BlockSpec((rows, width), lambda i: (i, 0))
        return pl.pallas_call(
            functools.partial(grads_kernel, own, groups),
            grid=(width // rows,),
            out_shape=(
                jax.ShapeDtypeStruct((own, model), BF),
                jax.ShapeDtypeStruct((width, units), BF),
                jax.ShapeDtypeStruct((width, units), BF),
                jax.ShapeDtypeStruct((units, width), BF),
            ),
            in_specs=[
                pl.BlockSpec((n_tok, rows), lambda i: (0, i)),
                full(n_tok, width),
                pl.BlockSpec((1, n_tok, rows), lambda i: (0, 0, i)),
                pl.BlockSpec((1, n_tok, units), lambda i: (1, 0, 0)),
                pl.BlockSpec((1, n_tok, units), lambda i: (2, 0, 0)),
                full(16, 16, 128),
            ],
            out_specs=(full(own, model), by_rows, by_rows, by_rows),
            scratch_shapes=[pltpu.VMEM((16, 16, 128), jnp.float32), pltpu.VMEM((8, model), jnp.float32)],
            compiler_params=pltpu.CompilerParams(vmem_limit_bytes=62 * 1024 * 1024),
        )(tok, grad, terms, terms, terms, ig)

    return on_device


def solution(mesh):
    sizes = mesh.shape
    shape = (sizes["depth"], sizes["row"], sizes["col"])
    on_device = fused(*shape) if shape == (4, 2, 4) else weight_stationary(*shape)
    return jax.shard_map(
        on_device,
        mesh=mesh,
        in_specs=(
            P(("depth", "row"), None),
            P(("depth", "row"), None),
            P("depth", ("row", "col")),
            P("depth", ("row", "col")),
            P(("row", "col"), "depth"),
        ),
        out_specs=(
            P(("depth", "row", "col"), None),
            P("depth", ("row", "col")),
            P("depth", ("row", "col")),
            P(("row", "col"), "depth"),
        ),
        check_vma=False,
    )
```
